256 devices in a mesh: seq: 64 (over z, x, y_lo), dp: 4 (over y_hi, core).
Axes of the slice: x: 4, y: 4 (y_hi: 2, y_lo: 2; y = y_hi * 2 + y_lo), z: 8, core: 2. Of those that a mesh axis runs over, the one named last changes fastest.
Arguments:
- tokens: bfloat16 [4, 65536, 512], P('dp', 'seq'), may hold values from -40 to 40
- cotangent: bfloat16 [4, 65536, 512], P('dp', 'seq'), may hold values from -16 to 16
- norm_gain: float32 [512], replicated, may hold values from 0.1 to 1.9
- gate_weight: float32 [512], replicated, may hold values from -4 to 4
- gate_bias: float32 [512], replicated, may hold values from -4 to 4
- first_factor: bfloat16 [512, 128, 128], P('seq'), may hold values from -0.5 to 0.5
- second_factor: bfloat16 [128, 4, 128, 128], P('seq'), may hold values from -0.5 to 0.5
- third_factor: bfloat16 [128, 4, 4, 128], P('seq'), may hold values from -3 to 3
- mlp_gain: float32 [512], replicated, may hold values from 0.1 to 1.9
- up_weight: bfloat16 [512, 2048], replicated, may hold values from -0.25 to 0.25
- down_weight: bfloat16 [2048, 512], replicated, may hold values from -0.125 to 0.125
Outputs:
- block_out: bfloat16 [4, 65536, 512], P('dp', 'seq')
- grad_tokens: bfloat16 [4, 65536, 512], P('dp', 'seq')
- grad_up: float32 [512, 2048], P(('seq', 'dp'))
- grad_down: float32 [512, 2048], P(('seq', 'dp'))
- grad_first: float32 [512, 128, 128], P('seq')
- grad_second: float32 [128, 4, 128, 128], P('seq')
- grad_third: float32 [128, 4, 4, 128], P('seq')
The draws below stay inside these ranges and needn't reach their ends.
All inputs are finite; a program needn't handle non-finite values.
Results may differ from the reference program's by a relative error of at most 0.018.
Values may be sent and summed in bfloat16 or wider, within the bound.
No kernel may reach another device: no remote copies, remote signals or barrier semaphores. Data moves between devices by JAX's collectives and lax.ppermute only.
A program may use at most 128 MiB of HBM per device.

```python
import math
import jax
import jax.numpy as jnp
from jax import lax

D = 512
FF = 2048
BLOCK = 128
MIDDLE = 128
OUTER = 4
LENGTH = 65536
SEQS = 4


def draw_tokens(key, part):
    base_key, row_key, col_key = jax.random.split(key, 3)
    base = jax.random.normal(base_key, (SEQS, LENGTH, D), jnp.float32)
    row_scale = jnp.exp(jax.random.uniform(row_key, (SEQS, LENGTH, 1), jnp.float32, math.log(1.0 / 3.0), math.log(3.0)))
    col_scale = jnp.exp(jax.random.uniform(col_key, (1, 1, D), jnp.float32, math.log(1.0 / 3.0), math.log(3.0)))
    return jnp.clip(base * row_scale * col_scale, -40.0, 40.0).astype(jnp.bfloat16)


def raised(drawn, own_key, source, target, blocks, factor):
    owner, partner = [(jnp.arange(drawn.shape[dim]) // (drawn.shape[dim] // blocks)).reshape([-1 if axis == dim else 1 for axis in range(drawn.ndim)]) for dim in (source, target)]
    chosen = jax.random.permutation(own_key, blocks)[partner]
    strong = (owner == chosen) | (owner == (partner + blocks // 2) % blocks)
    return jnp.where(strong, factor * drawn, drawn)


def shard_levels(stream_key, shape, cuts, least, high):
    loudness, own = 1.0, jax.random.fold_in(stream_key, 6)
    for position, shards_of in cuts:
        steps = jnp.exp(jax.random.uniform(jax.random.fold_in(own, position), (shards_of,), jnp.float32, least / len(cuts), high / len(cuts)))
        loudness = loudness * jnp.repeat(steps, shape[position] // shards_of).reshape([-1 if axis == position else 1 for axis in range(len(shape))])
    return loudness


def centred(rng, dims, scale, most, pieces=(), dtype=jnp.bfloat16):
    level = shard_levels(rng, dims, pieces, -0.22, 0.18) if pieces else 1.0
    values = jax.random.normal(rng, dims, jnp.float32) * scale * level
    return jnp.minimum(jnp.maximum(values, -most), most).astype(dtype)


def noise_with(stream_key, dims, spread, limit, cuts, heavy, held_as=jnp.bfloat16):
    array = spread * jax.random.normal(stream_key, dims, jnp.float32)
    if cuts:
        array = array * shard_levels(stream_key, dims, cuts, -0.22, 0.18)
    return jnp.clip(raised(array, jax.random.fold_in(stream_key, 3), *heavy), -limit, limit).astype(held_as)


def setup_inputs(seed: int = 0) -> dict:
    splits = jax.random.split(jax.random.key(seed), 12)
    tokens = draw_tokens(jax.random.fold_in(splits[11], 71), 0)
    cotangent = noise_with(splits[1], (SEQS, LENGTH, D), 1.0, 16.0, ((0, 4), (1, 64)), (1, 2, 64, 4.0))
    norm_gain = jnp.clip(1.0 + 0.18 * jax.random.normal(splits[2], (D,), jnp.float32), 0.1, 1.9)
    gate_weight = centred(splits[3], (D,), 1.0, 4.0, (), jnp.float32)
    gate_bias = centred(splits[4], (D,), 1.0, 4.0, (), jnp.float32)
    first_factor = centred(splits[5], (OUTER * MIDDLE, BLOCK, BLOCK), BLOCK ** -0.5, 0.5, ((0, 64),))
    second_factor = centred(splits[6], (BLOCK, OUTER, MIDDLE, MIDDLE), MIDDLE ** -0.5, 0.5, ((0, 64),))
    third_factor = centred(splits[7], (BLOCK, OUTER, OUTER, MIDDLE), OUTER ** -0.5, 3.0, ((0, 64),))
    mlp_gain = jnp.clip(1.0 + 0.18 * jax.random.normal(splits[8], (D,), jnp.float32), 0.1, 1.9)
    up_weight = centred(splits[9], (D, FF), D ** -0.5, 0.25)
    down_weight = centred(splits[10], (FF, D), FF ** -0.5, 0.125)
    return {"tokens": tokens, "cotangent": cotangent, "norm_gain": norm_gain, "gate_weight": gate_weight, "gate_bias": gate_bias, "first_factor": first_factor, "second_factor": second_factor, "third_factor": third_factor, "mlp_gain": mlp_gain, "up_weight": up_weight, "down_weight": down_weight}


epsilon = 1e-06
highest = lax.Precision.HIGHEST

def normalize(values, gain):
    inverse = lax.rsqrt(lax.optimization_barrier(jnp.mean(values * values, axis=-1, keepdims=True)) + epsilon)
    unit_part = values * inverse
    return (unit_part * gain, unit_part, inverse)

def norm_back(grad_in, unit_part, inverse, gain):
    scaled_grad = grad_in * gain
    return inverse * (scaled_grad - unit_part * lax.optimization_barrier(jnp.mean(scaled_grad * unit_part, axis=-1, keepdims=True)))

def gelu_tanh(values):
    return jax.nn.gelu(values, approximate=True)

def one_sequence(tokens_one, cot_one, norm_gain, gate_weight, gate_bias, first_factor, second_factor, third_factor, mlp_gain, up_weight, down_weight):
    f32 = jnp.float32
    bf16 = jnp.bfloat16
    tokens_flat = tokens_one.astype(f32)
    normed, unit_one, inverse_one = normalize(tokens_flat, norm_gain)
    mixer_in = normed.astype(bf16)
    input_grid = mixer_in.reshape(OUTER * MIDDLE, BLOCK, D)
    first_out = jnp.einsum('kpc,kcd->kpd', first_factor.astype(f32), input_grid.astype(f32), precision=highest).astype(bf16)
    first_cube = first_out.reshape(OUTER, MIDDLE, BLOCK, D)
    second_out = jnp.einsum('caqb,abcd->aqcd', second_factor.astype(f32), first_cube.astype(f32), precision=highest).astype(bf16)
    third_out = jnp.einsum('cqab,abcd->qbcd', third_factor.astype(f32), second_out.astype(f32), precision=highest).astype(bf16)
    mixed = third_out.reshape(LENGTH, D).astype(f32)
    gate_value = jax.nn.sigmoid(normed * gate_weight + gate_bias)
    hidden = (tokens_flat + gate_value * mixed).astype(bf16)
    hidden_wide = hidden.astype(f32)
    scaled, unit_two, inverse_two = normalize(hidden_wide, mlp_gain)
    scaled = scaled.astype(bf16)
    before = jnp.dot(scaled, up_weight, preferred_element_type=f32)
    act_value, act_back = jax.vjp(gelu_tanh, before)
    active = act_value.astype(bf16)
    block_out = (hidden_wide + jnp.dot(active, down_weight, preferred_element_type=f32)).astype(bf16)
    through = jnp.dot(cot_one, down_weight.T, preferred_element_type=f32)
    grad_pre = act_back(through)[0].astype(bf16)
    grad_down = jnp.dot(cot_one.T, active, preferred_element_type=f32)
    grad_up = jnp.dot(scaled.T, grad_pre, preferred_element_type=f32)
    grad_scaled = jnp.dot(grad_pre, up_weight.T, preferred_element_type=f32)
    grad_hidden = cot_one.astype(f32) + norm_back(grad_scaled, unit_two, inverse_two, mlp_gain)
    grad_mixed = (grad_hidden * gate_value).astype(bf16)
    gate_term = grad_hidden * mixed * gate_value * (1.0 - gate_value) * gate_weight
    grad_cube = grad_mixed.reshape(OUTER, MIDDLE, BLOCK, D)
    back_second = jnp.einsum('cqab,qbcd->abcd', third_factor.astype(f32), grad_cube.astype(f32), precision=highest).astype(bf16)
    grad_third = jnp.einsum('qbcd,abcd->cqab', grad_cube.astype(f32), second_out.astype(f32), precision=highest)
    back_first = jnp.einsum('caqb,aqcd->abcd', second_factor.astype(f32), back_second.astype(f32), precision=highest).astype(bf16)
    grad_second = jnp.einsum('aqcd,abcd->caqb', back_second.astype(f32), first_cube.astype(f32), precision=highest)
    back_rows = back_first.reshape(OUTER * MIDDLE, BLOCK, D)
    back_input = jnp.einsum('kpc,kpd->kcd', first_factor.astype(f32), back_rows.astype(f32), precision=highest).reshape(LENGTH, D)
    grad_first = jnp.einsum('kpd,kcd->kpc', back_rows.astype(f32), input_grid.astype(f32), precision=highest)
    grad_normed = back_input + gate_term
    grad_tokens = (grad_hidden + norm_back(grad_normed, unit_one, inverse_one, norm_gain)).astype(bf16)
    return (block_out, grad_tokens, grad_up, grad_down, grad_first, grad_second, grad_third)

def reference(tokens, cotangent, norm_gain, gate_weight, gate_bias, first_factor, second_factor, third_factor, mlp_gain, up_weight, down_weight):

    def apply_one(pair):
        return one_sequence(pair[0], pair[1], norm_gain, gate_weight, gate_bias, first_factor, second_factor, third_factor, mlp_gain, up_weight, down_weight)
    results = lax.map(apply_one, (tokens, cotangent))
    block_out, grad_tokens = (results[0], results[1])
    grad_up = lax.optimization_barrier(jnp.sum(results[2], axis=0))
    grad_down = lax.optimization_barrier(jnp.sum(results[3], axis=0))
    grad_first = lax.optimization_barrier(jnp.sum(results[4], axis=0))
    grad_second = lax.optimization_barrier(jnp.sum(results[5], axis=0))
    grad_third = lax.optimization_barrier(jnp.sum(results[6], axis=0))
    return (block_out, grad_tokens, grad_up, grad_down, grad_first, grad_second, grad_third)
```

```python
import jax
import jax.numpy as jnp
from jax import lax
from jax.experimental import pallas as pl
from jax.experimental.pallas import tpu as pltpu
from jax.sharding import PartitionSpec as P

f32 = jnp.float32
bf16 = jnp.bfloat16
epsilon = 1e-06
D = 512
FF = 2048
TILE = 512
GELU_SCALE = 0.7978845608028654
GELU_CUBE = 0.044715


def nn(a, b):
    return lax.dot_general(a, b, (((1,), (0,)), ((), ())), preferred_element_type=f32)


def nt(a, b):
    return lax.dot_general(a, b, (((1,), (1,)), ((), ())), preferred_element_type=f32)


def tn(a, b):
    return lax.dot_general(a, b, (((0,), (0,)), ((), ())), preferred_element_type=f32)


def iota(shape, dim):
    return lax.broadcasted_iota(jnp.int32, shape, dim)


def one_where(mask):
    return jnp.where(mask, 1.0, 0.0).astype(bf16)


def split_digit():
    row, col = iota((128, 128), 0), iota((128, 128), 1)
    return one_where(col == 2 * (row % 64) + row // 64)


def merge_digit():
    row, col = iota((128, 128), 0), iota((128, 128), 1)
    return one_where(row == 2 * (col % 64) + col // 64)


def spread_digit(e):
    row, col = iota((128, 256), 0), iota((128, 256), 1)
    return one_where((row == (col // 16) * 8 + col % 8) & ((col % 16) // 8 == e))


def inverse_of(values):
    return lax.rsqrt(jnp.mean(values * values, axis=-1, keepdims=True) + epsilon)


def norm_back(grad_in, unit_part, inverse, gain):
    scaled_grad = grad_in * gain
    return inverse * (
        scaled_grad - unit_part * jnp.mean(scaled_grad * unit_part, axis=-1, keepdims=True)
    )


def rows_of(k, size=128):
    return slice(k * size, (k + 1) * size)


def put_wire(wide_ref, k, values):
    for e in range(2):
        for lane in range(4):
            wide_ref[lane, pl.ds(e * 8 + k, 64, 16), :] = values[rows_of(e, 64), rows_of(lane)]


def get_wire(wide_ref, k):
    lanes = [
        jnp.concatenate([wide_ref[lane, pl.ds(e * 8 + k, 64, 16), :] for e in range(2)], axis=0)
        for lane in range(4)
    ]
    return jnp.concatenate(lanes, axis=1)


def to_wide(wide_ref, wire_ref):
    for lane in range(4):
        wide_ref[lane] = wire_ref[:, rows_of(lane)].astype(f32)


def from_wide(wire_ref, wide_ref):
    for lane in range(4):
        wire_ref[:, rows_of(lane)] = wide_ref[lane].astype(bf16)


WIDE = pltpu.VMEM((4, 1024, 128), f32)
PAIR = 2
PART = 256


def first_kernel(tokens_ref, gain_ref, factor_ref, wire_ref, wide_ref):
    step = pl.program_id(0)
    split = split_digit()
    for k in range(PAIR):
        values = tokens_ref[rows_of(k)].astype(f32)
        normed = values * inverse_of(values) * gain_ref[...]
        factor = nn(split, factor_ref[k]).astype(bf16)
        put_wire(wide_ref, step * PAIR + k, nn(factor, normed.astype(bf16)))

    @pl.when(step == pl.num_programs(0) - 1)
    def _():
        from_wide(wire_ref, wide_ref)


def gate_kernel(tokens_ref, gain_ref, weight_ref, bias_ref, gate_ref, input_ref):
    values = tokens_ref[...].astype(f32)
    normed = values * inverse_of(values) * gain_ref[...]
    input_ref[...] = normed.astype(bf16)
    gate = 0.5 + 0.5 * jnp.tanh(0.5 * (normed * weight_ref[...] + bias_ref[...]))
    gate_ref[...] = gate.astype(bf16)


def prepare_kernel(second_ref, third_ref, wide_factor_ref, columns_ref):
    spreads = [spread_digit(e) for e in range(2)]
    for a in range(4):
        total = jnp.zeros((256, 256), f32)
        for e in range(2):
            part = nn(second_ref[e, a], spreads[e]).astype(bf16)
            total = total + tn(spreads[e], part)
        wide_factor_ref[a] = total.astype(bf16)
    columns_ref[...] = tn(spreads[0], third_ref[0]) + tn(spreads[1], third_ref[1])


def mix_kernel(first_ref, factor_ref, columns_ref, second_ref, wire_ref):
    for a in range(4):
        rows = rows_of(a, 256)
        second_ref[rows] = nn(factor_ref[a], first_ref[rows]).astype(bf16)
    for q in range(4):
        total = None
        for a in range(4):
            index = q * 4 + a
            term = columns_ref[:, index : index + 1] * second_ref[rows_of(a, 256)].astype(f32)
            total = term if total is None else total + term
        wire_ref[rows_of(q, 256)] = total.astype(bf16)


def unmix_kernel(
    grad_ref, factor_ref, columns_ref, core_token_ref, second_ref, wire_ref, token_ref
):
    token_ref[...] = jnp.zeros_like(token_ref)
    for a in range(4):
        rows = rows_of(a, 256)
        total = None
        for q in range(4):
            index = q * 4 + a
            term = columns_ref[:, index : index + 1] * grad_ref[rows_of(q, 256)].astype(f32)
            total = term if total is None else total + term
        second = total.astype(bf16)
        second_ref[rows] = second
        wire_ref[rows] = tn(factor_ref[a], second).astype(bf16)


def factor_grad_kernel(grad_ref, second_ref, first_ref, back_ref, out_ref, token_ref):
    token_ref[...] = jnp.zeros_like(token_ref)
    spreads = [spread_digit(e) for e in range(2)]
    lane = iota((256, 128), 1)
    sums = jnp.zeros((256, 128), f32)
    for q in range(4):
        grad = grad_ref[rows_of(q, 256)].astype(f32)
        for a in range(4):
            product = grad * second_ref[rows_of(a, 256)].astype(f32)
            sums = jnp.where(lane == q * 4 + a, jnp.sum(product, axis=-1, keepdims=True), sums)
    sums = sums.astype(bf16)
    for e in range(2):
        out_ref[1024 + e * 16 : 1040 + e * 16] = tn(sums, spreads[e].T)[0:16].astype(bf16)
    for a in range(4):
        rows = rows_of(a, 256)
        wide = nt(back_ref[rows], first_ref[rows]).astype(bf16)
        for e in range(2):
            part = nn(spreads[e], wide).astype(bf16)
            out_ref[rows_of(e * 4 + a)] = nt(part, spreads[e]).astype(bf16)


def mlp_kernel(
    tokens_ref,
    cot_ref,
    wire_ref,
    gate_ref,
    through_ref,
    mlp_gain_ref,
    up_ref,
    hidden_ref,
    active_ref,
    grad_pre_ref,
    grad_hidden_ref,
    out_ref,
    wide_ref,
    scaled_ref,
    total_ref,
):
    step = pl.program_id(0)

    @pl.when(step == 0)
    def _():
        to_wide(wide_ref, wire_ref)
        merge = merge_digit()
        for k in range(8):
            rows = rows_of(k)
            mixed = nn(merge, get_wire(wide_ref, k).astype(bf16))
            gated = gate_ref[rows].astype(f32) * mixed
            hidden = (tokens_ref[rows].astype(f32) + gated).astype(bf16)
            hidden_ref[rows] = hidden
            hidden = hidden.astype(f32)
            scaled_ref[rows] = (hidden * inverse_of(hidden) * mlp_gain_ref[...]).astype(bf16)
        total_ref[...] = jnp.zeros_like(total_ref)

    up = up_ref[...]
    for part in range(1024 // PART):
        rows = rows_of(part, PART)
        value = nn(scaled_ref[rows], up)
        square = value * value
        tanh = jnp.tanh(value * (GELU_SCALE + (GELU_SCALE * GELU_CUBE) * square))
        outer = 0.5 + 0.5 * tanh
        active = value * outer
        slope = outer + active * (1.0 - outer) * (
            2.0 * GELU_SCALE + (6.0 * GELU_SCALE * GELU_CUBE) * square
        )
        active_ref[rows] = active.astype(bf16)
        grad_pre = (through_ref[rows].astype(f32) * slope).astype(bf16)
        grad_pre_ref[rows] = grad_pre
        total_ref[rows] += nt(grad_pre, up)

    @pl.when(step == pl.num_programs(0) - 1)
    def _():
        split = split_digit()
        for k in range(8):
            rows = rows_of(k)
            hidden = hidden_ref[rows].astype(f32)
            inverse = inverse_of(hidden)
            grad_hidden = cot_ref[rows].astype(f32) + norm_back(
                total_ref[rows], hidden * inverse, inverse, mlp_gain_ref[...]
            )
            grad_hidden_ref[rows] = grad_hidden.astype(bf16)
            gated = grad_hidden * gate_ref[rows].astype(f32)
            put_wire(wide_ref, k, nn(split, gated.astype(bf16)))
        from_wide(out_ref, wide_ref)


def owner_rows(place_ref):
    row, col = iota((512, 512), 0), iota((512, 512), 1)
    core = (row // 256 + place_ref[0]) % 2
    y = (row // 64 + place_ref[1]) % 4
    x = (row // 16 + place_ref[2]) % 4
    z = ((row // 2) % 8) ^ place_ref[3]
    return one_where(col == z * 64 + x * 16 + (y % 2) * 8 + (y // 2) * 4 + core * 2 + row % 2)


def through_kernel(place_ref, cot_ref, down_ref, through_ref, cot_t_ref):
    through_ref[...] = nt(cot_ref[...], down_ref[...]).astype(bf16)

    @pl.when(pl.program_id(0) == 0)
    def _():
        cot_t_ref[...] = nt(owner_rows(place_ref), cot_ref[...]).astype(bf16)


def weight_grad_kernel(
    place_ref,
    cot_t_ref,
    hidden_ref,
    mlp_gain_ref,
    active_ref,
    grad_pre_ref,
    keep_ref,
    send_up_ref,
    send_down_ref,
    scaled_t_ref,
):
    @pl.when(pl.program_id(0) == 0)
    def _():
        owner = owner_rows(place_ref)
        for part in range(4):
            rows = rows_of(part, 256)
            hidden = hidden_ref[rows].astype(f32)
            scaled = (hidden * inverse_of(hidden) * mlp_gain_ref[...]).astype(bf16)
            scaled_t_ref[:, rows] = nt(owner, scaled).astype(bf16)

    for index, (left_ref, right_ref, send_ref) in enumerate(
        ((scaled_t_ref, grad_pre_ref, send_up_ref), (cot_t_ref, active_ref, send_down_ref))
    ):
        keep_ref[index] = nn(left_ref[0:256], right_ref[...]).astype(bf16)
        send_ref[...] = nn(left_ref[256:512], right_ref[...]).astype(bf16)


def gate_term_kernel(
    wire_ref, gate_ref, gate_weight_ref, grad_hidden_ref, order_ref, term_ref, token_ref, wide_ref
):
    step = pl.program_id(0)

    @pl.when(step == 0)
    def _():
        to_wide(wide_ref, wire_ref)
        token_ref[...] = jnp.zeros_like(token_ref)

    merge = merge_digit()
    for k in range(PAIR):
        rows = rows_of(k)
        mixed = nn(merge, get_wire(wide_ref, step * PAIR + k).astype(bf16))
        gate = gate_ref[rows].astype(f32)
        slope = gate * (1.0 - gate) * gate_weight_ref[...]
        term_ref[rows] = grad_hidden_ref[rows].astype(f32) * mixed * slope


def first_grad_kernel(
    wire_ref, input_ref, factor_order_ref, term_order_ref, out_order_ref, out_ref, wide_ref
):
    step = pl.program_id(0)

    @pl.when(step == 0)
    def _():
        to_wide(wide_ref, wire_ref)

    merge = merge_digit()
    for k in range(PAIR):
        grad = get_wire(wide_ref, step * PAIR + k).astype(bf16)
        grad = nt(grad, input_ref[rows_of(k)]).astype(bf16)
        out_ref[rows_of(k)] = nn(merge, grad).astype(bf16)


def token_grad_kernel(
    wire_ref, tokens_ref, gain_ref, factor_ref, grad_hidden_ref, gate_term_ref, out_ref, wide_ref
):
    step = pl.program_id(0)

    @pl.when(step == 0)
    def _():
        to_wide(wide_ref, wire_ref)

    split = split_digit()
    for k in range(PAIR):
        rows = rows_of(k)
        values = tokens_ref[rows].astype(f32)
        inverse = inverse_of(values)
        factor = nn(split, factor_ref[k]).astype(bf16)
        back_input = tn(factor, get_wire(wide_ref, step * PAIR + k).astype(bf16))
        grad_normed = back_input + gate_term_ref[rows]
        out_ref[rows] = (
            grad_hidden_ref[rows].astype(f32)
            + norm_back(grad_normed, values * inverse, inverse, gain_ref[...])
        ).astype(bf16)


def shape(dims, dtype):
    return jax.ShapeDtypeStruct(dims, dtype)


def held(dims, dtype):
    return pltpu.HBM(dims, dtype)


def whole(*dims):
    return pl.BlockSpec(dims, lambda *_: (0,) * len(dims))


def row_blocks(rows, cols=D):
    return pl.BlockSpec((rows, cols), lambda i: (i, 0))


def col_blocks(rows, cols):
    return pl.BlockSpec((rows, cols), lambda i: (0, i))


def call(kernel, grid, in_specs, out_specs, out_shape, scratch, flops, moved, room):
    return pl.pallas_call(
        kernel,
        grid=(grid,),
        in_specs=in_specs,
        out_specs=out_specs,
        out_shape=out_shape,
        scratch_shapes=scratch,
        cost_estimate=pl.CostEstimate(flops=flops, bytes_accessed=moved, transcendentals=0),
        compiler_params=pltpu.CompilerParams(vmem_limit_bytes=room * 1024 * 1024),
    )


BOTH = ("seq", "dp")
SAME_CHIP = [(0, 1), (1, 0), (2, 3), (3, 2)]
FAR_CHIP = [(0, 2), (2, 0), (1, 3), (3, 1)]


def device_index(z, x, y, core):
    return ((z * 4 + x) * 2 + y % 2) * 4 + (y // 2) * 2 + core


def shift_pairs(axis, amount):
    pairs = []
    for z in range(8):
        for x in range(4):
            for y in range(4):
                for core in range(2):
                    target = {
                        "y": (z, x, (y + amount) % 4, core),
                        "x": (z, (x + amount) % 4, y, core),
                        "z": (z ^ amount, x, y, core),
                    }[axis]
                    pairs.append((device_index(z, x, y, core), device_index(*target)))
    return pairs


def add_parts(*parts):
    total = parts[0].astype(f32)
    for part in parts[1:]:
        total = total + part.astype(f32)
    return total


def core_sum_kernel(keep_ref, up_ref, down_ref, *refs):
    token_ref = refs[-1]
    for matrix, arrived_ref in enumerate((up_ref, down_ref)):
        for index in range(4):
            rows = rows_of(index, 64)
            total = keep_ref[matrix, rows].astype(f32) + arrived_ref[rows].astype(f32)
            refs[index][matrix] = total.astype(bf16)
    token_ref[...] = jnp.zeros_like(token_ref)


def plane_sum_kernel(token_ref, *refs):
    parts, results = refs[:4], refs[4:]
    for index, result_ref in enumerate(results):
        rows = rows_of(index, 16)
        for matrix in range(2):
            total = parts[0][matrix, rows].astype(f32)
            for part in parts[1:]:
                total = total + part[matrix, rows].astype(f32)
            result_ref[matrix] = total.astype(bf16)


def line_sum_kernel(order_ref, *refs):
    parts, results = refs[:-2], refs[-2:]
    rows = results[0].shape[1]
    for matrix in range(2):
        total = parts[0][matrix].astype(f32)
        for part in parts[1:]:
            total = total + part[matrix].astype(f32)
        for index, result_ref in enumerate(results):
            result_ref[matrix] = total[rows_of(index, rows)].astype(bf16)


def line_sum(parts, order):
    rows = parts[0].shape[1]
    return call(
        line_sum_kernel,
        1,
        [pl.BlockSpec(memory_space=pl.ANY)] + [whole(2, rows, FF)] * len(parts),
        [whole(2, rows // 2, FF)] * 2,
        [shape((2, rows // 2, FF), bf16)] * 2,
        [],
        1_000,
        1_000,
        8,
    )(order, *parts)


def send_around(blocks, axis):
    return [blocks[0]] + [
        lax.ppermute(blocks[amount], BOTH, shift_pairs(axis, amount))
        for amount in range(1, len(blocks))
    ]


def sequence_sum(part):
    part = add_parts(part, lax.ppermute(part, "dp", SAME_CHIP)).astype(bf16)
    return add_parts(part, lax.ppermute(part, "dp", FAR_CHIP)).astype(bf16)


def exchange(wire):
    return lax.all_to_all(wire, "seq", split_axis=0, concat_axis=0, tiled=True)


def local(
    tokens,
    cotangent,
    norm_gain,
    gate_weight,
    gate_bias,
    first_factor,
    second_factor,
    third_factor,
    mlp_gain,
    up_weight,
    down_weight,
):
    tokens = tokens.reshape(1024, D)
    cot = cotangent.reshape(1024, D)
    norm_gain, gate_weight, gate_bias, mlp_gain = (
        value.reshape(1, D) for value in (norm_gain, gate_weight, gate_bias, mlp_gain)
    )
    seq, dp = lax.axis_index("seq"), lax.axis_index("dp")
    place = jnp.stack(
        [dp & 1, (dp >> 1) * 2 + (seq & 1), (seq >> 1) & 3, seq >> 3]
    ).astype(jnp.int32)
    place_spec = pl.BlockSpec(memory_space=pltpu.SMEM)
    rows16, rows32 = shape((1024, D), bf16), shape((1024, D), f32)
    full, vector = whole(1024, D), whole(1, D)
    pair_rows = row_blocks(PAIR * 128)
    pair_factor = pl.BlockSpec((PAIR, 128, 128), lambda i: (i, 0, 0))
    steps = 8 // PAIR
    wide_columns = shape((1024, FF), bf16)
    held16, held_token = held((1024, D), bf16), held((16, 128), bf16)
    token_spec, token_shape = whole(16, 128), shape((16, 128), bf16)

    wire = call(
        first_kernel,
        steps,
        [pair_rows, vector, pair_factor],
        full,
        rows16,
        [WIDE],
        140_000_000,
        2_400_000,
        56,
    )(tokens, norm_gain, first_factor)
    first = exchange(wire)

    wide_factor, columns = call(
        prepare_kernel,
        1,
        [whole(2, 4, 128, 128), whole(2, 128, 16)],
        [whole(4, 256, 256), whole(256, 16)],
        [shape((4, 256, 256), bf16), shape((256, 16), f32)],
        [],
        200_000_000,
        1_000_000,
        24,
    )(second_factor, third_factor.reshape(2, 16, 128).transpose(0, 2, 1))
    gate, mixer_in = call(
        gate_kernel,
        4,
        [row_blocks(256), vector, vector, vector],
        [row_blocks(256), row_blocks(256)],
        [rows16, rows16],
        [],
        10_000_000,
        4_000_000,
        56,
    )(tokens, norm_gain, gate_weight, gate_bias)
    through, cot_t = call(
        through_kernel,
        FF // TILE,
        [place_spec, full, row_blocks(TILE)],
        [col_blocks(1024, TILE), whole(D, 1024)],
        [wide_columns, shape((D, 1024), bf16)],
        [],
        2_700_000_000,
        14_000_000,
        56,
    )(place, cot, down_weight)

    second, wire = call(
        mix_kernel,
        2,
        [col_blocks(1024, 256), whole(4, 256, 256), whole(256, 16)],
        [col_blocks(1024, 256), col_blocks(1024, 256)],
        [held16, held16],
        [],
        280_000_000,
        4_000_000,
        24,
    )(first, wide_factor, columns)
    wire = exchange(wire)

    mixed_wire = wire
    hidden, active, grad_pre, grad_hidden, wire = call(
        mlp_kernel,
        FF // TILE,
        [
            full,
            full,
            full,
            full,
            col_blocks(1024, TILE),
            vector,
            col_blocks(D, TILE),
        ],
        [full, col_blocks(1024, TILE), col_blocks(1024, TILE), full, full],
        [rows16, wide_columns, wide_columns, rows16, rows16],
        [WIDE, pltpu.VMEM((1024, D), bf16), pltpu.VMEM((1024, D), f32)],
        4_300_000_000,
        20_000_000,
        56,
    )(tokens, cot, wire, gate, through, mlp_gain, up_weight)
    grad_mixed = exchange(wire)

    keep, send_up, send_down = call(
        weight_grad_kernel,
        FF // TILE,
        [
            place_spec,
            whole(D, 1024),
            full,
            vector,
            col_blocks(1024, TILE),
            col_blocks(1024, TILE),
        ],
        [pl.BlockSpec((2, 256, TILE), lambda i: (0, 0, i))] + [col_blocks(256, TILE)] * 2,
        [shape((2, 256, FF), bf16)] + [shape((256, FF), bf16)] * 2,
        [pltpu.VMEM((D, 1024), bf16)],
        4_800_000_000,
        14_000_000,
        56,
    )(place, cot_t, hidden, mlp_gain, active, grad_pre)
    *blocks, core_token = call(
        core_sum_kernel,
        1,
        [whole(2, 256, FF), whole(256, FF), whole(256, FF)],
        [whole(2, 64, FF)] * 4 + [token_spec],
        [shape((2, 64, FF), bf16)] * 4 + [token_shape],
        [],
        1_000,
        1_000,
        56,
    )(keep, *(lax.ppermute(part, "dp", SAME_CHIP) for part in (send_up, send_down)))
    parts = send_around(blocks, "y")

    back_second, wire, token = call(
        unmix_kernel,
        2,
        [col_blocks(1024, 256), whole(4, 256, 256), whole(256, 16), token_spec],
        [col_blocks(1024, 256), col_blocks(1024, 256), token_spec],
        [held16, held16, held_token],
        [],
        1_000,
        1_000,
        24,
    )(grad_mixed, wide_factor, columns, core_token)
    back = exchange(wire)
    gate_term, term_token = call(
        gate_term_kernel,
        steps,
        [full, pair_rows, vector, pair_rows, token_spec],
        [pair_rows, token_spec],
        [rows32, token_shape],
        [WIDE],
        1_000_000,
        1_000,
        56,
    )(mixed_wire, gate, gate_weight, grad_hidden, token)
    block_out = (hidden.astype(f32) + nn(active, down_weight)).astype(bf16)
    factor_grads, factor_token = call(
        factor_grad_kernel,
        1,
        [full, full, full, full],
        [whole(1056, 128), token_spec],
        [shape((1056, 128), bf16), token_shape],
        [],
        1_000,
        1_000,
        56,
    )(grad_mixed, second, first, back_second)
    factor_grads = sequence_sum(factor_grads)

    blocks = call(
        plane_sum_kernel,
        1,
        [token_spec] + [whole(2, 64, FF)] * 4,
        [whole(2, 16, FF)] * 4,
        [shape((2, 16, FF), bf16)] * 4,
        [],
        1_000_000,
        2_500_000,
        16,
    )(token, *parts)
    parts = send_around(blocks, "x")
    parts = line_sum(parts, wire)
    parts = [parts[0], lax.ppermute(parts[1], BOTH, shift_pairs("z", 4))]
    parts = line_sum(parts, wire)
    parts = [parts[0], lax.ppermute(parts[1], BOTH, shift_pairs("z", 2))]
    parts = line_sum(parts, back)
    parts = [parts[0], lax.ppermute(parts[1], BOTH, shift_pairs("z", 1))]
    weight_grads = add_parts(*parts)

    grad_first = call(
        first_grad_kernel,
        steps,
        [full, pair_rows, token_spec, token_spec, pl.BlockSpec(memory_space=pl.ANY)],
        row_blocks(PAIR * 128, 128),
        shape((1024, 128), bf16),
        [WIDE],
        140_000_000,
        3_000_000,
        24,
    )(back, mixer_in, factor_token, term_token, block_out)
    grad_first = sequence_sum(grad_first)
    grad_tokens = call(
        token_grad_kernel,
        steps,
        [full, pair_rows, vector, pair_factor, pair_rows, pair_rows],
        pair_rows,
        rows16,
        [WIDE],
        140_000_000,
        8_000_000,
        24,
    )(back, tokens, norm_gain, first_factor, grad_hidden, gate_term)

    return (
        block_out.reshape(1, 1024, D),
        grad_tokens.reshape(1, 1024, D),
        weight_grads[0],
        weight_grads[1],
        grad_first.astype(f32).reshape(8, 128, 128),
        factor_grads[:1024].astype(f32).reshape(2, 4, 128, 128),
        factor_grads[1024:].astype(f32).reshape(2, 4, 4, 128),
    )


def solution(mesh):
    in_specs = (
        P("dp", "seq", None),
        P("dp", "seq", None),
        P(),
        P(),
        P(),
        P("seq", None, None),
        P("seq", None, None, None),
        P("seq", None, None, None),
        P(),
        P(),
        P(),
    )
    out_specs = (
        P("dp", "seq", None),
        P("dp", "seq", None),
        P(("seq", "dp"), None),
        P(("seq", "dp"), None),
        P("seq", None, None),
        P("seq", None, None, None),
        P("seq", None, None, None),
    )
    return jax.shard_map(local, mesh=mesh, in_specs=in_specs, out_specs=out_specs, check_vma=False)
```

```python
import jax
import jax.numpy as jnp
from jax import lax
from jax.experimental import pallas as pl
from jax.experimental.pallas import tpu as pltpu
from jax.sharding import PartitionSpec as P

f32 = jnp.float32
bf16 = jnp.bfloat16
epsilon = 1e-06
D = 512
FF = 2048
TILE = 512
GELU_SCALE = 0.7978845608028654
GELU_CUBE = 0.044715


def nn(a, b):
    return lax.dot_general(a, b, (((1,), (0,)), ((), ())), preferred_element_type=f32)


def nt(a, b):
    return lax.dot_general(a, b, (((1,), (1,)), ((), ())), preferred_element_type=f32)


def tn(a, b):
    return lax.dot_general(a, b, (((0,), (0,)), ((), ())), preferred_element_type=f32)


def iota(shape, dim):
    return lax.broadcasted_iota(jnp.int32, shape, dim)


def one_where(mask):
    return jnp.where(mask, 1.0, 0.0).astype(bf16)


def split_digit():
    row, col = iota((128, 128), 0), iota((128, 128), 1)
    return one_where(col == 2 * (row % 64) + row // 64)


def merge_digit():
    row, col = iota((128, 128), 0), iota((128, 128), 1)
    return one_where(row == 2 * (col % 64) + col // 64)


def spread_digit(e):
    row, col = iota((128, 256), 0), iota((128, 256), 1)
    return one_where((row == (col // 16) * 8 + col % 8) & ((col % 16) // 8 == e))


def inverse_of(values):
    return lax.rsqrt(jnp.mean(values * values, axis=-1, keepdims=True) + epsilon)


def norm_back(grad_in, unit_part, inverse, gain):
    scaled_grad = grad_in * gain
    return inverse * (
        scaled_grad - unit_part * jnp.mean(scaled_grad * unit_part, axis=-1, keepdims=True)
    )


def rows_of(k, size=128):
    return slice(k * size, (k + 1) * size)


def put_wire(wide_ref, k, values):
    for e in range(2):
        for lane in range(4):
            wide_ref[lane, pl.ds(e * 8 + k, 64, 16), :] = values[rows_of(e, 64), rows_of(lane)]


def get_wire(wide_ref, k):
    lanes = [
        jnp.concatenate([wide_ref[lane, pl.ds(e * 8 + k, 64, 16), :] for e in range(2)], axis=0)
        for lane in range(4)
    ]
    return jnp.concatenate(lanes, axis=1)


def to_wide(wide_ref, wire_ref):
    for lane in range(4):
        wide_ref[lane] = wire_ref[:, rows_of(lane)].astype(f32)


def from_wide(wire_ref, wide_ref):
    for lane in range(4):
        wire_ref[:, rows_of(lane)] = wide_ref[lane].astype(bf16)


WIDE = pltpu.VMEM((4, 1024, 128), f32)
PAIR = 2
WIDE_TILE = 1024


def first_kernel(tokens_ref, gain_ref, factor_ref, wire_ref, wide_ref):
    step = pl.program_id(0)
    split = split_digit()
    for k in range(PAIR):
        values = tokens_ref[rows_of(k)].astype(f32)
        normed = values * inverse_of(values) * gain_ref[...]
        factor = nn(split, factor_ref[k]).astype(bf16)
        put_wire(wide_ref, step * PAIR + k, nn(factor, normed.astype(bf16)))

    @pl.when(step == pl.num_programs(0) - 1)
    def _():
        from_wide(wire_ref, wide_ref)


def gate_kernel(tokens_ref, gain_ref, weight_ref, bias_ref, gate_ref, input_ref):
    values = tokens_ref[...].astype(f32)
    normed = values * inverse_of(values) * gain_ref[...]
    input_ref[...] = normed.astype(bf16)
    gate = 0.5 + 0.5 * jnp.tanh(0.5 * (normed * weight_ref[...] + bias_ref[...]))
    gate_ref[...] = gate.astype(bf16)


def prepare_kernel(second_ref, third_ref, wide_factor_ref, columns_ref):
    spreads = [spread_digit(e) for e in range(2)]
    for a in range(4):
        total = jnp.zeros((256, 256), f32)
        for e in range(2):
            part = nn(second_ref[e, a], spreads[e]).astype(bf16)
            total = total + tn(spreads[e], part)
        wide_factor_ref[a] = total.astype(bf16)
    columns_ref[...] = tn(spreads[0], third_ref[0]) + tn(spreads[1], third_ref[1])


def mix_kernel(first_ref, factor_ref, columns_ref, second_ref, wire_ref):
    for a in range(4):
        rows = rows_of(a, 256)
        second_ref[rows] = nn(factor_ref[a], first_ref[rows]).astype(bf16)
    for q in range(4):
        total = None
        for a in range(4):
            index = q * 4 + a
            term = columns_ref[:, index : index + 1] * second_ref[rows_of(a, 256)].astype(f32)
            total = term if total is None else total + term
        wire_ref[rows_of(q, 256)] = total.astype(bf16)


def unmix_kernel(
    grad_ref, factor_ref, columns_ref, core_token_ref, term_token_ref, second_ref, wire_ref, token_ref
):
    token_ref[...] = jnp.zeros_like(token_ref)
    for a in range(4):
        rows = rows_of(a, 256)
        total = None
        for q in range(4):
            index = q * 4 + a
            term = columns_ref[:, index : index + 1] * grad_ref[rows_of(q, 256)].astype(f32)
            total = term if total is None else total + term
        second = total.astype(bf16)
        second_ref[rows] = second
        wire_ref[rows] = tn(factor_ref[a], second).astype(bf16)


def factor_grad_kernel(grad_ref, second_ref, first_ref, back_ref, out_ref, token_ref):
    token_ref[...] = jnp.zeros_like(token_ref)
    spreads = [spread_digit(e) for e in range(2)]
    lane = iota((256, 128), 1)
    sums = jnp.zeros((256, 128), f32)
    for q in range(4):
        grad = grad_ref[rows_of(q, 256)].astype(f32)
        for a in range(4):
            product = grad * second_ref[rows_of(a, 256)].astype(f32)
            sums = jnp.where(lane == q * 4 + a, jnp.sum(product, axis=-1, keepdims=True), sums)
    sums = sums.astype(bf16)
    for e in range(2):
        out_ref[1024 + e * 16 : 1040 + e * 16] = tn(sums, spreads[e].T)[0:16].astype(bf16)
    for a in range(4):
        rows = rows_of(a, 256)
        wide = nt(back_ref[rows], first_ref[rows]).astype(bf16)
        for e in range(2):
            part = nn(spreads[e], wide).astype(bf16)
            out_ref[rows_of(e * 4 + a)] = nt(part, spreads[e]).astype(bf16)


def mlp_kernel(
    wire_hbm,
    tokens_hbm,
    gate_hbm,
    gain_hbm,
    up_hbm,
    through_hbm,
    cot_hbm,
    hidden_hbm,
    active_hbm,
    grad_pre_hbm,
    grad_hidden_hbm,
    out_hbm,
    wire_ref,
    tokens_ref,
    gate_ref,
    gain_ref,
    up_ref,
    through_ref,
    cot_ref,
    hidden_ref,
    active_ref,
    grad_pre_ref,
    grad_hidden_ref,
    wide_ref,
    scaled_ref,
    total_ref,
    in_sems,
    out_sems,
):
    sources = (wire_hbm, tokens_hbm, gate_hbm, gain_hbm, up_hbm, through_hbm, cot_hbm)
    targets = (wire_ref, tokens_ref, gate_ref, gain_ref, up_ref, through_ref, cot_ref)
    fetched = [
        pltpu.make_async_copy(source, target, in_sems.at[index])
        for index, (source, target) in enumerate(zip(sources, targets))
    ]
    for copy in fetched:
        copy.start()
    for copy in fetched[:4]:
        copy.wait()
    to_wide(wide_ref, wire_ref)
    merge, split = merge_digit(), split_digit()
    gain = gain_ref[...]
    stored = []

    def store(source, target):
        copy = pltpu.make_async_copy(source, target, out_sems.at[len(stored)])
        copy.start()
        stored.append(copy)

    for k in range(8):
        rows = rows_of(k)
        mixed = nn(merge, get_wire(wide_ref, k).astype(bf16))
        gated = gate_ref[rows].astype(f32) * mixed
        hidden = (tokens_ref[rows].astype(f32) + gated).astype(bf16)
        hidden_ref[rows] = hidden
        hidden = hidden.astype(f32)
        scaled_ref[rows] = (hidden * inverse_of(hidden) * gain).astype(bf16)
    store(hidden_ref, hidden_hbm)
    for copy in fetched[4:]:
        copy.wait()
    for step in range(FF // WIDE_TILE):
        cols = slice(step * WIDE_TILE, (step + 1) * WIDE_TILE)
        up = up_ref[:, cols]
        value = nn(scaled_ref[...], up)
        square = value * value
        tanh = jnp.tanh(value * (GELU_SCALE + (GELU_SCALE * GELU_CUBE) * square))
        outer = 0.5 + 0.5 * tanh
        active = value * outer
        slope = outer + active * (1.0 - outer) * (
            2.0 * GELU_SCALE + (6.0 * GELU_SCALE * GELU_CUBE) * square
        )
        active_ref[:, cols] = active.astype(bf16)
        grad_pre = (through_ref[:, cols].astype(f32) * slope).astype(bf16)
        grad_pre_ref[:, cols] = grad_pre
        store(active_ref.at[:, cols], active_hbm.at[:, cols])
        store(grad_pre_ref.at[:, cols], grad_pre_hbm.at[:, cols])
        total = nt(grad_pre, up)
        if step == 0:
            total_ref[...] = total
        else:
            total_ref[...] += total
    for k in range(8):
        rows = rows_of(k)
        hidden = hidden_ref[rows].astype(f32)
        inverse = inverse_of(hidden)
        grad_hidden = cot_ref[rows].astype(f32) + norm_back(
            total_ref[rows], hidden * inverse, inverse, gain
        )
        grad_hidden_ref[rows] = grad_hidden.astype(bf16)
        gated = grad_hidden * gate_ref[rows].astype(f32)
        put_wire(wide_ref, k, nn(split, gated.astype(bf16)))
    store(grad_hidden_ref, grad_hidden_hbm)
    from_wide(wire_ref, wide_ref)
    store(wire_ref, out_hbm)
    for copy in stored:
        copy.wait()


def owner_rows(place_ref):
    row, col = iota((512, 512), 0), iota((512, 512), 1)
    core = (row // 256 + place_ref[0]) % 2
    y = (row // 64 + place_ref[1]) % 4
    x = (row // 16 + place_ref[2]) % 4
    z = ((row // 2) % 8) ^ place_ref[3]
    return one_where(col == z * 64 + x * 16 + (y % 2) * 8 + (y // 2) * 4 + core * 2 + row % 2)


def through_kernel(place_ref, cot_ref, down_ref, through_ref, cot_t_ref):
    through_ref[...] = nt(cot_ref[...], down_ref[...]).astype(bf16)

    @pl.when(pl.program_id(0) == 0)
    def _():
        cot_t_ref[...] = nt(owner_rows(place_ref), cot_ref[...]).astype(bf16)


def weight_grad_kernel(
    place_ref,
    cot_t_ref,
    hidden_ref,
    mlp_gain_ref,
    active_ref,
    grad_pre_ref,
    keep_ref,
    send_up_ref,
    send_down_ref,
    scaled_t_ref,
):
    @pl.when(pl.program_id(0) == 0)
    def _():
        owner = owner_rows(place_ref)
        for part in range(4):
            rows = rows_of(part, 256)
            hidden = hidden_ref[rows].astype(f32)
            scaled = (hidden * inverse_of(hidden) * mlp_gain_ref[...]).astype(bf16)
            scaled_t_ref[:, rows] = nt(owner, scaled).astype(bf16)

    for index, (left_ref, right_ref, send_ref) in enumerate(
        ((scaled_t_ref, grad_pre_ref, send_up_ref), (cot_t_ref, active_ref, send_down_ref))
    ):
        product = nn(left_ref[...], right_ref[...]).astype(bf16)
        keep_ref[index] = product[0:256]
        send_ref[...] = product[256:512]


def gate_term_kernel(
    wire_ref, gate_ref, gate_weight_ref, grad_hidden_ref, term_ref, token_ref, wide_ref
):
    step = pl.program_id(0)

    @pl.when(step == 0)
    def _():
        to_wide(wide_ref, wire_ref)
        token_ref[...] = jnp.zeros_like(token_ref)

    merge = merge_digit()
    for k in range(PAIR):
        rows = rows_of(k)
        mixed = nn(merge, get_wire(wide_ref, step * PAIR + k).astype(bf16))
        gate = gate_ref[rows].astype(f32)
        slope = gate * (1.0 - gate) * gate_weight_ref[...]
        term_ref[rows] = grad_hidden_ref[rows].astype(f32) * mixed * slope


def first_grad_kernel(
    wire_ref, input_ref, factor_order_ref, out_order_ref, out_ref, wide_ref
):
    step = pl.program_id(0)

    @pl.when(step == 0)
    def _():
        to_wide(wide_ref, wire_ref)

    merge = merge_digit()
    for k in range(PAIR):
        grad = get_wire(wide_ref, step * PAIR + k).astype(bf16)
        grad = nt(grad, input_ref[rows_of(k)]).astype(bf16)
        out_ref[rows_of(k)] = nn(merge, grad).astype(bf16)


def token_grad_kernel(
    wire_ref, tokens_ref, gain_ref, factor_ref, grad_hidden_ref, gate_term_ref, out_ref, wide_ref
):
    step = pl.program_id(0)

    @pl.when(step == 0)
    def _():
        to_wide(wide_ref, wire_ref)

    split = split_digit()
    for k in range(PAIR):
        rows = rows_of(k)
        values = tokens_ref[rows].astype(f32)
        inverse = inverse_of(values)
        factor = nn(split, factor_ref[k]).astype(bf16)
        back_input = tn(factor, get_wire(wide_ref, step * PAIR + k).astype(bf16))
        grad_normed = back_input + gate_term_ref[rows]
        out_ref[rows] = (
            grad_hidden_ref[rows].astype(f32)
            + norm_back(grad_normed, values * inverse, inverse, gain_ref[...])
        ).astype(bf16)


def shape(dims, dtype):
    return jax.ShapeDtypeStruct(dims, dtype)


def held(dims, dtype):
    return pltpu.HBM(dims, dtype)


def whole(*dims):
    return pl.BlockSpec(dims, lambda *_: (0,) * len(dims))


def row_blocks(rows, cols=D):
    return pl.BlockSpec((rows, cols), lambda i: (i, 0))


def col_blocks(rows, cols):
    return pl.BlockSpec((rows, cols), lambda i: (0, i))


def call(kernel, grid, in_specs, out_specs, out_shape, scratch, flops, moved, room):
    return pl.pallas_call(
        kernel,
        grid=(grid,),
        in_specs=in_specs,
        out_specs=out_specs,
        out_shape=out_shape,
        scratch_shapes=scratch,
        cost_estimate=pl.CostEstimate(flops=flops, bytes_accessed=moved, transcendentals=0),
        compiler_params=pltpu.CompilerParams(vmem_limit_bytes=room * 1024 * 1024),
    )


BOTH = ("seq", "dp")
SAME_CHIP = [(0, 1), (1, 0), (2, 3), (3, 2)]
FAR_CHIP = [(0, 2), (2, 0), (1, 3), (3, 1)]


def device_index(z, x, y, core):
    return ((z * 4 + x) * 2 + y % 2) * 4 + (y // 2) * 2 + core


def shift_pairs(axis, amount):
    pairs = []
    for z in range(8):
        for x in range(4):
            for y in range(4):
                for core in range(2):
                    target = {
                        "y": (z, x, (y + amount) % 4, core),
                        "x": (z, (x + amount) % 4, y, core),
                        "z": (z ^ amount, x, y, core),
                    }[axis]
                    pairs.append((device_index(z, x, y, core), device_index(*target)))
    return pairs


def add_parts(*parts):
    total = parts[0].astype(f32)
    for part in parts[1:]:
        total = total + part.astype(f32)
    return total


def core_sum_kernel(keep_ref, up_ref, down_ref, *refs):
    token_ref = refs[-1]
    for matrix, arrived_ref in enumerate((up_ref, down_ref)):
        for index in range(4):
            rows = rows_of(index, 64)
            total = keep_ref[matrix, rows].astype(f32) + arrived_ref[rows].astype(f32)
            refs[index][matrix] = total.astype(bf16)
    token_ref[...] = jnp.zeros_like(token_ref)


def plane_sum_kernel(token_ref, *refs):
    parts, results = refs[:4], refs[4:]
    for index, result_ref in enumerate(results):
        rows = rows_of(index, 16)
        for matrix in range(2):
            total = parts[0][matrix, rows].astype(f32)
            for part in parts[1:]:
                total = total + part[matrix, rows].astype(f32)
            result_ref[matrix] = total.astype(bf16)


def line_sum_kernel(order_ref, *refs):
    parts, results = refs[:-2], refs[-2:]
    rows = results[0].shape[1]
    for matrix in range(2):
        total = parts[0][matrix].astype(f32)
        for part in parts[1:]:
            total = total + part[matrix].astype(f32)
        for index, result_ref in enumerate(results):
            result_ref[matrix] = total[rows_of(index, rows)].astype(bf16)


def line_sum(parts, order):
    rows = parts[0].shape[1]
    return call(
        line_sum_kernel,
        1,
        [pl.BlockSpec(memory_space=pl.ANY)] + [whole(2, rows, FF)] * len(parts),
        [whole(2, rows // 2, FF)] * 2,
        [shape((2, rows // 2, FF), bf16)] * 2,
        [],
        1_000,
        1_000,
        8,
    )(order, *parts)


def send_around(blocks, axis):
    return [blocks[0]] + [
        lax.ppermute(blocks[amount], BOTH, shift_pairs(axis, amount))
        for amount in range(1, len(blocks))
    ]


def sequence_sum(part):
    part = add_parts(part, lax.ppermute(part, "dp", SAME_CHIP)).astype(bf16)
    return add_parts(part, lax.ppermute(part, "dp", FAR_CHIP)).astype(bf16)


def exchange(wire):
    return lax.all_to_all(wire, "seq", split_axis=0, concat_axis=0, tiled=True)


def local(
    tokens,
    cotangent,
    norm_gain,
    gate_weight,
    gate_bias,
    first_factor,
    second_factor,
    third_factor,
    mlp_gain,
    up_weight,
    down_weight,
):
    tokens = tokens.reshape(1024, D)
    cot = cotangent.reshape(1024, D)
    norm_gain, gate_weight, gate_bias, mlp_gain = (
        value.reshape(1, D) for value in (norm_gain, gate_weight, gate_bias, mlp_gain)
    )
    seq, dp = lax.axis_index("seq"), lax.axis_index("dp")
    place = jnp.stack(
        [dp & 1, (dp >> 1) * 2 + (seq & 1), (seq >> 1) & 3, seq >> 3]
    ).astype(jnp.int32)
    place_spec = pl.BlockSpec(memory_space=pltpu.SMEM)
    rows16, rows32 = shape((1024, D), bf16), shape((1024, D), f32)
    full, vector = whole(1024, D), whole(1, D)
    pair_rows = row_blocks(PAIR * 128)
    pair_factor = pl.BlockSpec((PAIR, 128, 128), lambda i: (i, 0, 0))
    steps = 8 // PAIR
    wide_columns = shape((1024, FF), bf16)
    held16, held_token = held((1024, D), bf16), held((16, 128), bf16)
    held_wide = held((1024, FF), bf16)
    token_spec, token_shape = whole(16, 128), shape((16, 128), bf16)

    wire = call(
        first_kernel,
        steps,
        [pair_rows, vector, pair_factor],
        full,
        rows16,
        [WIDE],
        140_000_000,
        2_400_000,
        56,
    )(tokens, norm_gain, first_factor)
    first = exchange(wire)

    wide_factor, columns = call(
        prepare_kernel,
        1,
        [whole(2, 4, 128, 128), whole(2, 128, 16)],
        [whole(4, 256, 256), whole(256, 16)],
        [shape((4, 256, 256), bf16), shape((256, 16), f32)],
        [],
        200_000_000,
        1_000_000,
        24,
    )(second_factor, third_factor.reshape(2, 16, 128).transpose(0, 2, 1))
    gate, mixer_in = call(
        gate_kernel,
        4,
        [row_blocks(256), vector, vector, vector],
        [row_blocks(256), row_blocks(256)],
        [rows16, rows16],
        [],
        10_000_000,
        4_000_000,
        56,
    )(tokens, norm_gain, gate_weight, gate_bias)
    through, cot_t = call(
        through_kernel,
        FF // TILE,
        [place_spec, full, row_blocks(TILE)],
        [col_blocks(1024, TILE), whole(D, 1024)],
        [wide_columns, shape((D, 1024), bf16)],
        [],
        2_700_000_000,
        14_000_000,
        56,
    )(place, cot, down_weight)

    second, wire = call(
        mix_kernel,
        2,
        [col_blocks(1024, 256), whole(4, 256, 256), whole(256, 16)],
        [col_blocks(1024, 256), col_blocks(1024, 256)],
        [held16, held16],
        [],
        280_000_000,
        4_000_000,
        24,
    )(first, wide_factor, columns)
    wire = exchange(wire)

    mixed_wire = wire
    pinned = pl.BlockSpec(memory_space=pltpu.HBM)
    room16, room_wide = pltpu.VMEM((1024, D), bf16), pltpu.VMEM((1024, FF), bf16)
    hidden, active, grad_pre, grad_hidden, wire = call(
        mlp_kernel,
        1,
        [pl.BlockSpec(memory_space=pl.ANY)] + [pinned] * 6,
        [pinned] * 5,
        [held16, held_wide, held_wide, held16, held16],
        [
            room16,
            room16,
            room16,
            pltpu.VMEM((1, D), f32),
            pltpu.VMEM((D, FF), bf16),
            room_wide,
            room16,
            room16,
            room_wide,
            room_wide,
            room16,
            WIDE,
            room16,
            pltpu.VMEM((1024, D), f32),
            pltpu.SemaphoreType.DMA((7,)),
            pltpu.SemaphoreType.DMA((3 + 2 * (FF // WIDE_TILE),)),
        ],
        4_300_000_000,
        20_000_000,
        56,
    )(wire, tokens, gate, mlp_gain, up_weight, through, cot)
    grad_mixed = exchange(wire)

    keep, send_up, send_down = call(
        weight_grad_kernel,
        FF // TILE,
        [
            place_spec,
            whole(D, 1024),
            full,
            vector,
            col_blocks(1024, TILE),
            col_blocks(1024, TILE),
        ],
        [pl.BlockSpec((2, 256, TILE), lambda i: (0, 0, i))] + [col_blocks(256, TILE)] * 2,
        [shape((2, 256, FF), bf16)] + [shape((256, FF), bf16)] * 2,
        [pltpu.VMEM((D, 1024), bf16)],
        4_800_000_000,
        14_000_000,
        56,
    )(place, cot_t, hidden, mlp_gain, active, grad_pre)
    gate_term, term_token = call(
        gate_term_kernel,
        steps,
        [full, pair_rows, vector, pair_rows],
        [pair_rows, token_spec],
        [rows32, token_shape],
        [WIDE],
        1_000_000,
        1_000,
        56,
    )(mixed_wire, gate, gate_weight, grad_hidden)
    *blocks, core_token = call(
        core_sum_kernel,
        1,
        [whole(2, 256, FF), whole(256, FF), whole(256, FF)],
        [whole(2, 64, FF)] * 4 + [token_spec],
        [shape((2, 64, FF), bf16)] * 4 + [token_shape],
        [],
        1_000,
        1_000,
        56,
    )(keep, *(lax.ppermute(part, "dp", SAME_CHIP) for part in (send_up, send_down)))
    parts = send_around(blocks, "y")

    back_second, wire, token = call(
        unmix_kernel,
        2,
        [col_blocks(1024, 256), whole(4, 256, 256), whole(256, 16), token_spec, token_spec],
        [col_blocks(1024, 256), col_blocks(1024, 256), token_spec],
        [held16, held16, held_token],
        [],
        1_000,
        1_000,
        24,
    )(grad_mixed, wide_factor, columns, core_token, term_token)
    back = exchange(wire)
    block_out = (hidden.astype(f32) + nn(active, down_weight)).astype(bf16)
    factor_grads, factor_token = call(
        factor_grad_kernel,
        1,
        [full, full, full, full],
        [whole(1056, 128), token_spec],
        [shape((1056, 128), bf16), token_shape],
        [],
        1_000,
        1_000,
        56,
    )(grad_mixed, second, first, back_second)
    factor_grads = sequence_sum(factor_grads)

    blocks = call(
        plane_sum_kernel,
        1,
        [token_spec] + [whole(2, 64, FF)] * 4,
        [whole(2, 16, FF)] * 4,
        [shape((2, 16, FF), bf16)] * 4,
        [],
        1_000_000,
        2_500_000,
        16,
    )(token, *parts)
    parts = send_around(blocks, "x")
    parts = line_sum(parts, wire)
    parts = [parts[0], lax.ppermute(parts[1], BOTH, shift_pairs("z", 4))]
    parts = line_sum(parts, wire)
    parts = [parts[0], lax.ppermute(parts[1], BOTH, shift_pairs("z", 2))]
    parts = line_sum(parts, back)
    parts = [parts[0], lax.ppermute(parts[1], BOTH, shift_pairs("z", 1))]
    weight_grads = add_parts(*parts)

    grad_first = call(
        first_grad_kernel,
        steps,
        [full, pair_rows, token_spec, pl.BlockSpec(memory_space=pl.ANY)],
        row_blocks(PAIR * 128, 128),
        shape((1024, 128), bf16),
        [WIDE],
        140_000_000,
        3_000_000,
        24,
    )(back, mixer_in, factor_token, block_out)
    grad_first = sequence_sum(grad_first)
    grad_tokens = call(
        token_grad_kernel,
        steps,
        [full, pair_rows, vector, pair_factor, pair_rows, pair_rows],
        pair_rows,
        rows16,
        [WIDE],
        140_000_000,
        8_000_000,
        24,
    )(back, tokens, norm_gain, first_factor, grad_hidden, gate_term)

    return (
        block_out.reshape(1, 1024, D),
        grad_tokens.reshape(1, 1024, D),
        weight_grads[0],
        weight_grads[1],
        grad_first.astype(f32).reshape(8, 128, 128),
        factor_grads[:1024].astype(f32).reshape(2, 4, 128, 128),
        factor_grads[1024:].astype(f32).reshape(2, 4, 4, 128),
    )


def solution(mesh):
    in_specs = (
        P("dp", "seq", None),
        P("dp", "seq", None),
        P(),
        P(),
        P(),
        P("seq", None, None),
        P("seq", None, None, None),
        P("seq", None, None, None),
        P(),
        P(),
        P(),
    )
    out_specs = (
        P("dp", "seq", None),
        P("dp", "seq", None),
        P(("seq", "dp"), None),
        P(("seq", "dp"), None),
        P("seq", None, None),
        P("seq", None, None, None),
        P("seq", None, None, None),
    )
    return jax.shard_map(local, mesh=mesh, in_specs=in_specs, out_specs=out_specs, check_vma=False)
```

```python
import jax
import jax.numpy as jnp
from jax import lax
from jax.experimental import pallas as pl
from jax.experimental.pallas import tpu as pltpu
from jax.sharding import PartitionSpec as P

f32 = jnp.float32
bf16 = jnp.bfloat16
epsilon = 1e-06
D = 512
FF = 2048
TILE = 512
GELU_SCALE = 0.7978845608028654
GELU_CUBE = 0.044715


def nn(a, b):
    return lax.dot_general(a, b, (((1,), (0,)), ((), ())), preferred_element_type=f32)


def nt(a, b):
    return lax.dot_general(a, b, (((1,), (1,)), ((), ())), preferred_element_type=f32)


def tn(a, b):
    return lax.dot_general(a, b, (((0,), (0,)), ((), ())), preferred_element_type=f32)


def iota(shape, dim):
    return lax.broadcasted_iota(jnp.int32, shape, dim)


def one_where(mask):
    return jnp.where(mask, 1.0, 0.0).astype(bf16)


def split_digit():
    row, col = iota((128, 128), 0), iota((128, 128), 1)
    return one_where(col == 2 * (row % 64) + row // 64)


def merge_digit():
    row, col = iota((128, 128), 0), iota((128, 128), 1)
    return one_where(row == 2 * (col % 64) + col // 64)


def spread_digit(e):
    row, col = iota((128, 256), 0), iota((128, 256), 1)
    return one_where((row == (col // 16) * 8 + col % 8) & ((col % 16) // 8 == e))


def inverse_of(values):
    return lax.rsqrt(jnp.mean(values * values, axis=-1, keepdims=True) + epsilon)


def norm_back(grad_in, unit_part, inverse, gain):
    scaled_grad = grad_in * gain
    return inverse * (
        scaled_grad - unit_part * jnp.mean(scaled_grad * unit_part, axis=-1, keepdims=True)
    )


def rows_of(k, size=128):
    return slice(k * size, (k + 1) * size)


def put_wire(wide_ref, k, values):
    for e in range(2):
        for lane in range(4):
            wide_ref[lane, pl.ds(e * 8 + k, 64, 16), :] = values[rows_of(e, 64), rows_of(lane)]


def get_wire(wide_ref, k):
    lanes = [
        jnp.concatenate([wide_ref[lane, pl.ds(e * 8 + k, 64, 16), :] for e in range(2)], axis=0)
        for lane in range(4)
    ]
    return jnp.concatenate(lanes, axis=1)


def to_wide(wide_ref, wire_ref):
    for lane in range(4):
        wide_ref[lane] = wire_ref[:, rows_of(lane)].astype(f32)


def from_wide(wire_ref, wide_ref):
    for lane in range(4):
        wire_ref[:, rows_of(lane)] = wide_ref[lane].astype(bf16)


WIDE = pltpu.VMEM((4, 1024, 128), f32)
PAIR = 2
WIDE_TILE = 1024


def first_kernel(tokens_ref, gain_ref, factor_ref, wire_ref, wide_ref):
    step = pl.program_id(0)
    split = split_digit()
    for k in range(PAIR):
        values = tokens_ref[rows_of(k)].astype(f32)
        normed = values * inverse_of(values) * gain_ref[...]
        factor = nn(split, factor_ref[k]).astype(bf16)
        put_wire(wide_ref, step * PAIR + k, nn(factor, normed.astype(bf16)))

    @pl.when(step == pl.num_programs(0) - 1)
    def _():
        from_wide(wire_ref, wide_ref)


def gate_kernel(tokens_ref, gain_ref, weight_ref, bias_ref, gate_ref, input_ref):
    values = tokens_ref[...].astype(f32)
    normed = values * inverse_of(values) * gain_ref[...]
    input_ref[...] = normed.astype(bf16)
    gate = 0.5 + 0.5 * jnp.tanh(0.5 * (normed * weight_ref[...] + bias_ref[...]))
    gate_ref[...] = gate.astype(bf16)


def prepare_kernel(second_ref, third_ref, wide_factor_ref, columns_ref):
    spreads = [spread_digit(e) for e in range(2)]
    for a in range(4):
        total = jnp.zeros((256, 256), f32)
        for e in range(2):
            part = nn(second_ref[e, a], spreads[e]).astype(bf16)
            total = total + tn(spreads[e], part)
        wide_factor_ref[a] = total.astype(bf16)
    columns_ref[...] = tn(spreads[0], third_ref[0]) + tn(spreads[1], third_ref[1])


def mix_kernel(first_ref, factor_ref, columns_ref, second_ref, wire_ref):
    for a in range(4):
        rows = rows_of(a, 256)
        second_ref[rows] = nn(factor_ref[a], first_ref[rows]).astype(bf16)
    for q in range(4):
        total = None
        for a in range(4):
            index = q * 4 + a
            term = columns_ref[:, index : index + 1] * second_ref[rows_of(a, 256)].astype(f32)
            total = term if total is None else total + term
        wire_ref[rows_of(q, 256)] = total.astype(bf16)


def unmix_kernel(
    grad_ref, factor_ref, columns_ref, core_token_ref, second_ref, wire_ref, token_ref
):
    token_ref[...] = jnp.zeros_like(token_ref)
    for a in range(4):
        rows = rows_of(a, 256)
        total = None
        for q in range(4):
            index = q * 4 + a
            term = columns_ref[:, index : index + 1] * grad_ref[rows_of(q, 256)].astype(f32)
            total = term if total is None else total + term
        second = total.astype(bf16)
        second_ref[rows] = second
        wire_ref[rows] = tn(factor_ref[a], second).astype(bf16)


def factor_grad_kernel(grad_ref, second_ref, first_ref, back_ref, out_ref, token_ref):
    token_ref[...] = jnp.zeros_like(token_ref)
    spreads = [spread_digit(e) for e in range(2)]
    lane = iota((256, 128), 1)
    sums = jnp.zeros((256, 128), f32)
    for q in range(4):
        grad = grad_ref[rows_of(q, 256)].astype(f32)
        for a in range(4):
            product = grad * second_ref[rows_of(a, 256)].astype(f32)
            sums = jnp.where(lane == q * 4 + a, jnp.sum(product, axis=-1, keepdims=True), sums)
    sums = sums.astype(bf16)
    for e in range(2):
        out_ref[1024 + e * 16 : 1040 + e * 16] = tn(sums, spreads[e].T)[0:16].astype(bf16)
    for a in range(4):
        rows = rows_of(a, 256)
        wide = nt(back_ref[rows], first_ref[rows]).astype(bf16)
        for e in range(2):
            part = nn(spreads[e], wide).astype(bf16)
            out_ref[rows_of(e * 4 + a)] = nt(part, spreads[e]).astype(bf16)


def mlp_kernel(
    wire_hbm,
    tokens_hbm,
    gate_hbm,
    gain_hbm,
    weight_hbm,
    up_hbm,
    through_hbm,
    cot_hbm,
    hidden_hbm,
    active_hbm,
    grad_pre_hbm,
    grad_hidden_hbm,
    slope_hbm,
    out_hbm,
    wire_ref,
    tokens_ref,
    gate_ref,
    gain_ref,
    weight_ref,
    up_ref,
    through_ref,
    cot_ref,
    hidden_ref,
    active_ref,
    grad_pre_ref,
    grad_hidden_ref,
    slope_ref,
    wide_ref,
    scaled_ref,
    total_ref,
    in_sems,
    out_sems,
):
    sources = (
        wire_hbm, tokens_hbm, gate_hbm, gain_hbm, weight_hbm, up_hbm, through_hbm, cot_hbm
    )
    targets = (
        wire_ref, tokens_ref, gate_ref, gain_ref, weight_ref, up_ref, through_ref, cot_ref
    )
    fetched = [
        pltpu.make_async_copy(source, target, in_sems.at[index])
        for index, (source, target) in enumerate(zip(sources, targets))
    ]
    for copy in fetched:
        copy.start()
    for copy in fetched[:5]:
        copy.wait()
    to_wide(wide_ref, wire_ref)
    merge, split = merge_digit(), split_digit()
    gain = gain_ref[...]
    stored = []

    def store(source, target):
        copy = pltpu.make_async_copy(source, target, out_sems.at[len(stored)])
        copy.start()
        stored.append(copy)

    for k in range(8):
        rows = rows_of(k)
        mixed = nn(merge, get_wire(wide_ref, k).astype(bf16))
        gate = gate_ref[rows].astype(f32)
        gated = gate * mixed
        slope_ref[rows] = (gated * (1.0 - gate) * weight_ref[...]).astype(bf16)
        hidden = (tokens_ref[rows].astype(f32) + gated).astype(bf16)
        hidden_ref[rows] = hidden
        hidden = hidden.astype(f32)
        scaled_ref[rows] = (hidden * inverse_of(hidden) * gain).astype(bf16)
    store(hidden_ref, hidden_hbm)
    store(slope_ref, slope_hbm)
    for copy in fetched[5:]:
        copy.wait()
    for step in range(FF // WIDE_TILE):
        cols = slice(step * WIDE_TILE, (step + 1) * WIDE_TILE)
        up = up_ref[:, cols]
        value = nn(scaled_ref[...], up)
        square = value * value
        tanh = jnp.tanh(value * (GELU_SCALE + (GELU_SCALE * GELU_CUBE) * square))
        outer = 0.5 + 0.5 * tanh
        active = value * outer
        slope = outer + active * (1.0 - outer) * (
            2.0 * GELU_SCALE + (6.0 * GELU_SCALE * GELU_CUBE) * square
        )
        active_ref[:, cols] = active.astype(bf16)
        grad_pre = (through_ref[:, cols].astype(f32) * slope).astype(bf16)
        grad_pre_ref[:, cols] = grad_pre
        store(active_ref.at[:, cols], active_hbm.at[:, cols])
        store(grad_pre_ref.at[:, cols], grad_pre_hbm.at[:, cols])
        total = nt(grad_pre, up)
        if step == 0:
            total_ref[...] = total
        else:
            total_ref[...] += total
    for k in range(8):
        rows = rows_of(k)
        hidden = hidden_ref[rows].astype(f32)
        inverse = inverse_of(hidden)
        grad_hidden = cot_ref[rows].astype(f32) + norm_back(
            total_ref[rows], hidden * inverse, inverse, gain
        )
        grad_hidden_ref[rows] = grad_hidden.astype(bf16)
        gated = grad_hidden * gate_ref[rows].astype(f32)
        put_wire(wide_ref, k, nn(split, gated.astype(bf16)))
    store(grad_hidden_ref, grad_hidden_hbm)
    from_wide(wire_ref, wide_ref)
    store(wire_ref, out_hbm)
    for copy in stored:
        copy.wait()


def owner_rows(place_ref):
    row, col = iota((512, 512), 0), iota((512, 512), 1)
    core = (row // 256 + place_ref[0]) % 2
    y = (row // 64 + place_ref[1]) % 4
    x = (row // 16 + place_ref[2]) % 4
    z = ((row // 2) % 8) ^ place_ref[3]
    return one_where(col == z * 64 + x * 16 + (y % 2) * 8 + (y // 2) * 4 + core * 2 + row % 2)


def through_kernel(place_ref, cot_ref, down_ref, through_ref, cot_t_ref):
    through_ref[...] = nt(cot_ref[...], down_ref[...]).astype(bf16)

    @pl.when(pl.program_id(0) == 0)
    def _():
        cot_t_ref[...] = nt(owner_rows(place_ref), cot_ref[...]).astype(bf16)


def weight_grad_kernel(
    place_ref,
    cot_t_ref,
    hidden_ref,
    mlp_gain_ref,
    active_ref,
    grad_pre_ref,
    keep_ref,
    send_up_ref,
    send_down_ref,
    scaled_t_ref,
):
    @pl.when(pl.program_id(0) == 0)
    def _():
        owner = owner_rows(place_ref)
        for part in range(4):
            rows = rows_of(part, 256)
            hidden = hidden_ref[rows].astype(f32)
            scaled = (hidden * inverse_of(hidden) * mlp_gain_ref[...]).astype(bf16)
            scaled_t_ref[:, rows] = nt(owner, scaled).astype(bf16)

    for index, (left_ref, right_ref, send_ref) in enumerate(
        ((scaled_t_ref, grad_pre_ref, send_up_ref), (cot_t_ref, active_ref, send_down_ref))
    ):
        product = nn(left_ref[...], right_ref[...]).astype(bf16)
        keep_ref[index] = product[0:256]
        send_ref[...] = product[256:512]


def first_grad_kernel(
    wire_ref, input_ref, factor_order_ref, out_order_ref, out_ref, wide_ref
):
    step = pl.program_id(0)

    @pl.when(step == 0)
    def _():
        to_wide(wide_ref, wire_ref)

    merge = merge_digit()
    for k in range(PAIR):
        grad = get_wire(wide_ref, step * PAIR + k).astype(bf16)
        grad = nt(grad, input_ref[rows_of(k)]).astype(bf16)
        out_ref[rows_of(k)] = nn(merge, grad).astype(bf16)


def token_grad_kernel(
    wire_ref, tokens_ref, gain_ref, factor_ref, grad_hidden_ref, slope_ref, out_ref, wide_ref
):
    step = pl.program_id(0)

    @pl.when(step == 0)
    def _():
        to_wide(wide_ref, wire_ref)

    split = split_digit()
    for k in range(PAIR):
        rows = rows_of(k)
        values = tokens_ref[rows].astype(f32)
        inverse = inverse_of(values)
        factor = nn(split, factor_ref[k]).astype(bf16)
        back_input = tn(factor, get_wire(wide_ref, step * PAIR + k).astype(bf16))
        grad_hidden = grad_hidden_ref[rows].astype(f32)
        grad_normed = back_input + grad_hidden * slope_ref[rows].astype(f32)
        out_ref[rows] = (
            grad_hidden
            + norm_back(grad_normed, values * inverse, inverse, gain_ref[...])
        ).astype(bf16)


def shape(dims, dtype):
    return jax.ShapeDtypeStruct(dims, dtype)


def held(dims, dtype):
    return pltpu.HBM(dims, dtype)


def whole(*dims):
    return pl.BlockSpec(dims, lambda *_: (0,) * len(dims))


def row_blocks(rows, cols=D):
    return pl.BlockSpec((rows, cols), lambda i: (i, 0))


def col_blocks(rows, cols):
    return pl.BlockSpec((rows, cols), lambda i: (0, i))


def call(kernel, grid, in_specs, out_specs, out_shape, scratch, flops, moved, room):
    return pl.pallas_call(
        kernel,
        grid=(grid,),
        in_specs=in_specs,
        out_specs=out_specs,
        out_shape=out_shape,
        scratch_shapes=scratch,
        cost_estimate=pl.CostEstimate(flops=flops, bytes_accessed=moved, transcendentals=0),
        compiler_params=pltpu.CompilerParams(vmem_limit_bytes=room * 1024 * 1024),
    )


BOTH = ("seq", "dp")
SAME_CHIP = [(0, 1), (1, 0), (2, 3), (3, 2)]
FAR_CHIP = [(0, 2), (2, 0), (1, 3), (3, 1)]


def device_index(z, x, y, core):
    return ((z * 4 + x) * 2 + y % 2) * 4 + (y // 2) * 2 + core


def shift_pairs(axis, amount):
    pairs = []
    for z in range(8):
        for x in range(4):
            for y in range(4):
                for core in range(2):
                    target = {
                        "y": (z, x, (y + amount) % 4, core),
                        "x": (z, (x + amount) % 4, y, core),
                        "z": (z ^ amount, x, y, core),
                    }[axis]
                    pairs.append((device_index(z, x, y, core), device_index(*target)))
    return pairs


def add_parts(*parts):
    total = parts[0].astype(f32)
    for part in parts[1:]:
        total = total + part.astype(f32)
    return total


def core_sum_kernel(keep_ref, up_ref, down_ref, *refs):
    token_ref = refs[-1]
    for matrix, arrived_ref in enumerate((up_ref, down_ref)):
        for index in range(4):
            rows = rows_of(index, 64)
            total = keep_ref[matrix, rows].astype(f32) + arrived_ref[rows].astype(f32)
            refs[index][matrix] = total.astype(bf16)
    token_ref[...] = jnp.zeros_like(token_ref)


def plane_sum_kernel(token_ref, *refs):
    parts, results = refs[:4], refs[4:]
    for index, result_ref in enumerate(results):
        rows = rows_of(index, 16)
        for matrix in range(2):
            total = parts[0][matrix, rows].astype(f32)
            for part in parts[1:]:
                total = total + part[matrix, rows].astype(f32)
            result_ref[matrix] = total.astype(bf16)


def line_sum_kernel(order_ref, *refs):
    parts, results = refs[:-2], refs[-2:]
    rows = results[0].shape[1]
    for matrix in range(2):
        total = parts[0][matrix].astype(f32)
        for part in parts[1:]:
            total = total + part[matrix].astype(f32)
        for index, result_ref in enumerate(results):
            result_ref[matrix] = total[rows_of(index, rows)].astype(bf16)


def line_sum(parts, order):
    rows = parts[0].shape[1]
    return call(
        line_sum_kernel,
        1,
        [pl.BlockSpec(memory_space=pl.ANY)] + [whole(2, rows, FF)] * len(parts),
        [whole(2, rows // 2, FF)] * 2,
        [shape((2, rows // 2, FF), bf16)] * 2,
        [],
        1_000,
        1_000,
        8,
    )(order, *parts)


def send_around(blocks, axis):
    return [blocks[0]] + [
        lax.ppermute(blocks[amount], BOTH, shift_pairs(axis, amount))
        for amount in range(1, len(blocks))
    ]


def sequence_sum(part):
    part = add_parts(part, lax.ppermute(part, "dp", SAME_CHIP)).astype(bf16)
    return add_parts(part, lax.ppermute(part, "dp", FAR_CHIP))


def exchange(wire):
    return lax.all_to_all(wire, "seq", split_axis=0, concat_axis=0, tiled=True)


def local(
    tokens,
    cotangent,
    norm_gain,
    gate_weight,
    gate_bias,
    first_factor,
    second_factor,
    third_factor,
    mlp_gain,
    up_weight,
    down_weight,
):
    tokens = tokens.reshape(1024, D)
    cot = cotangent.reshape(1024, D)
    norm_gain, gate_weight, gate_bias, mlp_gain = (
        value.reshape(1, D) for value in (norm_gain, gate_weight, gate_bias, mlp_gain)
    )
    seq, dp = lax.axis_index("seq"), lax.axis_index("dp")
    place = jnp.stack(
        [dp & 1, (dp >> 1) * 2 + (seq & 1), (seq >> 1) & 3, seq >> 3]
    ).astype(jnp.int32)
    place_spec = pl.BlockSpec(memory_space=pltpu.SMEM)
    rows16, rows32 = shape((1024, D), bf16), shape((1024, D), f32)
    full, vector = whole(1024, D), whole(1, D)
    pair_rows = row_blocks(PAIR * 128)
    pair_factor = pl.BlockSpec((PAIR, 128, 128), lambda i: (i, 0, 0))
    steps = 8 // PAIR
    wide_columns = shape((1024, FF), bf16)
    held16, held_token = held((1024, D), bf16), held((16, 128), bf16)
    held_wide = held((1024, FF), bf16)
    token_spec, token_shape = whole(16, 128), shape((16, 128), bf16)

    wire = call(
        first_kernel,
        steps,
        [pair_rows, vector, pair_factor],
        full,
        rows16,
        [WIDE],
        140_000_000,
        2_400_000,
        56,
    )(tokens, norm_gain, first_factor)
    first = exchange(wire)

    wide_factor, columns = call(
        prepare_kernel,
        1,
        [whole(2, 4, 128, 128), whole(2, 128, 16)],
        [whole(4, 256, 256), whole(256, 16)],
        [shape((4, 256, 256), bf16), shape((256, 16), f32)],
        [],
        200_000_000,
        1_000_000,
        24,
    )(second_factor, third_factor.reshape(2, 16, 128).transpose(0, 2, 1))
    gate, mixer_in = call(
        gate_kernel,
        4,
        [row_blocks(256), vector, vector, vector],
        [row_blocks(256), row_blocks(256)],
        [rows16, rows16],
        [],
        10_000_000,
        4_000_000,
        56,
    )(tokens, norm_gain, gate_weight, gate_bias)
    through, cot_t = call(
        through_kernel,
        FF // TILE,
        [place_spec, full, row_blocks(TILE)],
        [col_blocks(1024, TILE), whole(D, 1024)],
        [wide_columns, shape((D, 1024), bf16)],
        [],
        2_700_000_000,
        14_000_000,
        56,
    )(place, cot, down_weight)

    second, wire = call(
        mix_kernel,
        2,
        [col_blocks(1024, 256), whole(4, 256, 256), whole(256, 16)],
        [col_blocks(1024, 256), col_blocks(1024, 256)],
        [held16, held16],
        [],
        280_000_000,
        4_000_000,
        24,
    )(first, wide_factor, columns)
    wire = exchange(wire)

    pinned = pl.BlockSpec(memory_space=pltpu.HBM)
    room16, room_wide = pltpu.VMEM((1024, D), bf16), pltpu.VMEM((1024, FF), bf16)
    hidden, active, grad_pre, grad_hidden, gate_slope, wire = call(
        mlp_kernel,
        1,
        [pl.BlockSpec(memory_space=pl.ANY)] + [pinned] * 7,
        [pinned] * 6,
        [held16, held_wide, held_wide, held16, held16, held16],
        [
            room16,
            room16,
            room16,
            pltpu.VMEM((1, D), f32),
            pltpu.VMEM((1, D), f32),
            pltpu.VMEM((D, FF), bf16),
            room_wide,
            room16,
            room16,
            room_wide,
            room_wide,
            room16,
            room16,
            WIDE,
            room16,
            pltpu.VMEM((1024, D), f32),
            pltpu.SemaphoreType.DMA((8,)),
            pltpu.SemaphoreType.DMA((4 + 2 * (FF // WIDE_TILE),)),
        ],
        4_300_000_000,
        20_000_000,
        56,
    )(wire, tokens, gate, mlp_gain, gate_weight, up_weight, through, cot)
    grad_mixed = exchange(wire)

    keep, send_up, send_down = call(
        weight_grad_kernel,
        FF // TILE,
        [
            place_spec,
            whole(D, 1024),
            full,
            vector,
            col_blocks(1024, TILE),
            col_blocks(1024, TILE),
        ],
        [pl.BlockSpec((2, 256, TILE), lambda i: (0, 0, i))] + [col_blocks(256, TILE)] * 2,
        [shape((2, 256, FF), bf16)] + [shape((256, FF), bf16)] * 2,
        [pltpu.VMEM((D, 1024), bf16)],
        4_800_000_000,
        14_000_000,
        56,
    )(place, cot_t, hidden, mlp_gain, active, grad_pre)
    *blocks, core_token = call(
        core_sum_kernel,
        1,
        [whole(2, 256, FF), whole(256, FF), whole(256, FF)],
        [whole(2, 64, FF)] * 4 + [token_spec],
        [shape((2, 64, FF), bf16)] * 4 + [token_shape],
        [],
        1_000,
        1_000,
        20,
    )(keep, *(lax.ppermute(part, "dp", SAME_CHIP) for part in (send_up, send_down)))
    parts = send_around(blocks, "y")

    back_second, wire, token = call(
        unmix_kernel,
        2,
        [col_blocks(1024, 256), whole(4, 256, 256), whole(256, 16), token_spec],
        [col_blocks(1024, 256), col_blocks(1024, 256), token_spec],
        [held16, held16, held_token],
        [],
        1_000,
        1_000,
        24,
    )(grad_mixed, wide_factor, columns, core_token)
    back = exchange(wire)
    factor_grads, factor_token = call(
        factor_grad_kernel,
        1,
        [full, full, full, full],
        [whole(1056, 128), token_spec],
        [shape((1056, 128), bf16), token_shape],
        [],
        1_000,
        1_000,
        56,
    )(grad_mixed, second, first, back_second)
    factor_grads = sequence_sum(factor_grads)

    blocks = call(
        plane_sum_kernel,
        1,
        [token_spec] + [whole(2, 64, FF)] * 4,
        [whole(2, 16, FF)] * 4,
        [shape((2, 16, FF), bf16)] * 4,
        [],
        1_000_000,
        2_500_000,
        16,
    )(token, *parts)
    parts = send_around(blocks, "x")
    block_out = (hidden.astype(f32) + nn(active, down_weight)).astype(bf16)
    parts = line_sum(parts, block_out)
    parts = [parts[0], lax.ppermute(parts[1], BOTH, shift_pairs("z", 4))]
    parts = line_sum(parts, wire)
    parts = [parts[0], lax.ppermute(parts[1], BOTH, shift_pairs("z", 2))]
    parts = line_sum(parts, back)
    parts = [parts[0], lax.ppermute(parts[1], BOTH, shift_pairs("z", 1))]
    weight_grads = add_parts(*parts)

    grad_first = call(
        first_grad_kernel,
        steps,
        [full, pair_rows, token_spec, pl.BlockSpec(memory_space=pl.ANY)],
        row_blocks(PAIR * 128, 128),
        shape((1024, 128), bf16),
        [WIDE],
        140_000_000,
        3_000_000,
        24,
    )(back, mixer_in, factor_token, block_out)
    grad_first = sequence_sum(grad_first)
    grad_tokens = call(
        token_grad_kernel,
        steps,
        [full, pair_rows, vector, pair_factor, pair_rows, pair_rows],
        pair_rows,
        rows16,
        [WIDE],
        140_000_000,
        8_000_000,
        24,
    )(back, tokens, norm_gain, first_factor, grad_hidden, gate_slope)

    return (
        block_out.reshape(1, 1024, D),
        grad_tokens.reshape(1, 1024, D),
        weight_grads[0],
        weight_grads[1],
        grad_first.reshape(8, 128, 128),
        factor_grads[:1024].reshape(2, 4, 128, 128),
        factor_grads[1024:].reshape(2, 4, 4, 128),
    )


def solution(mesh):
    in_specs = (
        P("dp", "seq", None),
        P("dp", "seq", None),
        P(),
        P(),
        P(),
        P("seq", None, None),
        P("seq", None, None, None),
        P("seq", None, None, None),
        P(),
        P(),
        P(),
    )
    out_specs = (
        P("dp", "seq", None),
        P("dp", "seq", None),
        P(("seq", "dp"), None),
        P(("seq", "dp"), None),
        P("seq", None, None),
        P("seq", None, None, None),
        P("seq", None, None, None),
    )
    return jax.shard_map(local, mesh=mesh, in_specs=in_specs, out_specs=out_specs, check_vma=False)
```
